1024 devices in a mesh: sec: 256 (over y, z, x_hi, core), row: 4 (over x_lo).
Axes of the slice: x: 8 (x_hi: 2, x_lo: 4; x = x_hi * 4 + x_lo), y: 8, z: 8, core: 2. Of those that a mesh axis runs over, the one named last changes fastest.
Arguments:
- section_images: bfloat16 [256, 512, 512], P('sec', 'row'), may hold values from -6 to 6
- displacement: float32 [2, 256, 4, 4], P(None, 'sec', 'row'), may hold values from -2 to 2
- fold_mask: int32 [2, 256, 4, 4], P(None, 'sec', 'row'), may hold values 0 or 1
Outputs:
- relaxed_field: float32 [2, 256, 4, 4], P(None, 'sec', 'row')
- mean_offsets: float32 [2, 256, 4, 4], P(None, 'sec', 'row')
The draws below stay inside these ranges and needn't reach their ends.
All inputs are finite; a program needn't handle non-finite values. No bound on the sum of `fold_mask` on one device may be relied on, other than what follows from the above.
Results may differ from the reference program's by a relative error of at most 0.0003.
Values may be sent and summed in bfloat16 or wider, within the bound.
A program may use at most 32 MiB of HBM per device.

```python
import math
import jax
import jax.numpy as jnp
from jax import lax

PATCH = 128
COLS = 512
ITERS = 3
SECTIONS = 256
NROWS = 512
PROWS = 4
PCOLS = 4


def with_ends(drawn, stream_key, low, high):
    longest = drawn.shape.index(max(drawn.shape))
    spots = []
    for shift in (0, 1):
        where = [jax.random.randint(jax.random.fold_in(stream_key, axis), (), 0, length) for axis, length in enumerate(drawn.shape)]
        where[longest] = (where[longest] + shift) % drawn.shape[longest]
        spots.append(tuple(where))
    return drawn.at[spots[0]].set(low).at[spots[1]].set(high)


def level_of(rng, dims, cuts, smallest, high):
    loudness = 1.0
    for dim, shards_of in cuts:
        draws = jax.random.uniform(jax.random.fold_in(jax.random.fold_in(rng, 6), dim), (shards_of,), jnp.float32, smallest / len(cuts), high / len(cuts))
        loudness = loudness * jnp.repeat(jnp.exp(draws), dims[dim] // shards_of).reshape((-1,) + (1,) * (len(dims) - 1 - dim))
    return loudness


def gaussian(own_key, shape, width, most, cuts=(), kind=jnp.bfloat16):
    drawn = jax.random.normal(own_key, shape, jnp.float32) * width
    if len(cuts) > 0:
        drawn = level_of(own_key, shape, cuts, -0.22, 0.18) * drawn
    return jnp.clip(drawn, min=-most, max=most).astype(kind)


def setup_inputs(seed: int = 0) -> dict:
    seeds = jax.random.split(jax.random.key(seed), 4)
    return {
        "section_images": gaussian(seeds[0], (SECTIONS, NROWS, COLS), 1.0, 6.0, ((0, 256), (1, 4))),
        "displacement": jnp.clip(jax.random.uniform(seeds[1], (2, SECTIONS, PROWS, PCOLS), jnp.float32, -2.0, 2.0) * level_of(seeds[1], (2, SECTIONS, PROWS, PCOLS), ((1, 256), (2, 4)), -0.4, 0.0), -2.0, 2.0),
        "fold_mask": with_ends((jax.random.randint(seeds[2], (2, SECTIONS, PROWS, PCOLS), 0, 4) < 3).astype(jnp.int32), jax.random.fold_in(seeds[2], 1), 0, 1),
    }


step_size = 0.5
stiffness = 0.2
epsilon = 1e-06
highest = lax.Precision.HIGHEST

def dft_tables(size):
    indices = jnp.arange(size, dtype=jnp.int32)
    products = indices[:, None] * indices[None, :] % size
    angles = products.astype(jnp.float32) * (2.0 * math.pi / size)
    signed = (indices - size * (indices >= size // 2).astype(jnp.int32)).astype(jnp.float32)
    nonzero = 1.0 - ((indices[:, None] == 0) & (indices[None, :] == 0)).astype(jnp.float32)
    return (jnp.cos(angles), jnp.sin(angles), signed, nonzero[None, :, :, None])

def to_patches(section_plane, size):
    rows_total, cols_total = section_plane.shape
    values = section_plane.astype(jnp.float32).reshape(rows_total // size, size, cols_total // size, size)
    return jnp.transpose(values, (0, 1, 3, 2))

def along_first(matrix, values):
    return jnp.einsum('uy,ryxc->ruxc', matrix, values, precision=highest)

def along_second(matrix, values):
    return jnp.einsum('vx,ruxc->ruvc', matrix, values, precision=highest)

def forward(values, tables):
    cosines, sines = (tables[0], tables[1])
    first_real = along_first(cosines, values)
    first_imag = -along_first(sines, values)
    real_part = along_second(cosines, first_real) + along_second(sines, first_imag)
    imag_part = along_second(cosines, first_imag) - along_second(sines, first_real)
    return (real_part, imag_part)

def inverse_real(real_part, imag_part, tables):
    cosines, sines = (tables[0], tables[1])
    size = cosines.shape[0]
    first_real = along_first(cosines, real_part) - along_first(sines, imag_part)
    first_imag = along_first(cosines, imag_part) + along_first(sines, real_part)
    return (along_second(cosines, first_real) - along_second(sines, first_imag)) / float(size * size)

def warp(spectrum, shifts, tables):
    cosines, sines, signed, nonzero = tables
    size = cosines.shape[0]
    phases = -2.0 * math.pi / size * (signed[None, :, None, None] * shifts[0][:, None, None, :] + signed[None, None, :, None] * shifts[1][:, None, None, :])
    rotate_real = jnp.cos(phases) * nonzero
    rotate_imag = jnp.sin(phases) * nonzero
    new_real = spectrum[0] * rotate_real - spectrum[1] * rotate_imag
    new_imag = spectrum[0] * rotate_imag + spectrum[1] * rotate_real
    return inverse_real(new_real, new_imag, tables)

def spectrum_energy(warped, tables):
    return (forward(warped, tables), lax.optimization_barrier(jnp.sum(warped * warped, axis=(1, 2), keepdims=True)))

def correlate(own_spectrum, own_energy, other_spectrum, other_energy, tables):
    signed = tables[2]
    sharpness = 0.5 * float(tables[0].shape[0])
    cross_real = own_spectrum[0] * other_spectrum[0] + own_spectrum[1] * other_spectrum[1]
    cross_imag = own_spectrum[1] * other_spectrum[0] - own_spectrum[0] * other_spectrum[1]
    lagged = inverse_real(cross_real, cross_imag, tables)
    scores = sharpness * lagged / jnp.sqrt(own_energy * other_energy + epsilon)
    weights = jnp.exp(scores)
    totals = lax.optimization_barrier(jnp.sum(weights, axis=(1, 2)))
    offset_rows = lax.optimization_barrier(jnp.sum(weights * signed[None, :, None, None], axis=(1, 2))) / totals
    offset_cols = lax.optimization_barrier(jnp.sum(weights * signed[None, None, :, None], axis=(1, 2))) / totals
    return jnp.stack([offset_rows, offset_cols])

def combine_terms(own_terms, below_terms, above_terms, lower_weight, upper_weight, tables):
    offset_lower = correlate(own_terms[0], own_terms[1], below_terms[0], below_terms[1], tables)
    offset_upper = correlate(own_terms[0], own_terms[1], above_terms[0], above_terms[1], tables)
    return (lower_weight * offset_lower + upper_weight * offset_upper) / jnp.maximum(lower_weight + upper_weight, 1.0)

def smooth(padded, current):
    neighbours = padded[:, :, :-2, 1:-1] + padded[:, :, 2:, 1:-1] + padded[:, :, 1:-1, :-2] + padded[:, :, 1:-1, 2:]
    return current + stiffness * (neighbours - 4.0 * current)

def reference(section_images, displacement, fold_mask):
    tables = dft_tables(PATCH)
    section_total = section_images.shape[0]
    mask_values = fold_mask.astype(jnp.float32)
    current = displacement
    averaged = jnp.zeros_like(displacement)
    section_ids = jnp.arange(section_total, dtype=jnp.int32)
    for iteration in range(ITERS):

        def warp_one(section, current=current):
            section_plane = lax.dynamic_index_in_dim(section_images, section, 0, keepdims=False)
            shifts = lax.dynamic_index_in_dim(current, section, 1, keepdims=False)
            warped = warp(forward(to_patches(section_plane, PATCH), tables), shifts, tables)
            return spectrum_energy(warped, tables)
        all_terms = lax.map(warp_one, section_ids)

        def per_section(section_index, all_terms=all_terms):
            lower_index = jnp.maximum(section_index - 1, 0).astype(jnp.int32)
            upper_index = jnp.minimum(section_index + 1, section_total - 1).astype(jnp.int32)

            def pick(section):
                return jax.tree.map(lambda leaf: lax.dynamic_index_in_dim(leaf, section, 0, keepdims=False), all_terms)
            lower_weight = lax.dynamic_index_in_dim(mask_values[0], section_index, 0, keepdims=False) * (section_index > 0).astype(jnp.float32)
            upper_weight = lax.dynamic_index_in_dim(mask_values[1], section_index, 0, keepdims=False) * (section_index < section_total - 1).astype(jnp.float32)
            return combine_terms(pick(section_index), pick(lower_index), pick(upper_index), lower_weight, upper_weight, tables)
        averaged = jnp.transpose(lax.map(per_section, section_ids), (1, 0, 2, 3))
        updated = current + step_size * averaged
        padded = jnp.pad(updated, ((0, 0), (0, 0), (1, 1), (1, 1)))
        current = smooth(padded, updated)
    return (current, averaged)
```

```python
import functools
import math

import jax
import jax.numpy as jnp
import numpy as np
from jax import lax
from jax.experimental import pallas as pl
from jax.experimental.pallas import tpu as pltpu
from jax.sharding import PartitionSpec as P

SIZE = 128
HALF = 64
ITERS = 3
STEP = 0.5
STIFF = 0.2
EPS = 1e-6
SHARP = 0.5 * SIZE
F32 = jnp.float32
BF16 = jnp.bfloat16
COORD = pl.DeviceIdType.MESH

NEAR = [(1, 0), (-1, 0)]
PEERS = NEAR + [(0, 1), (0, -1), (1, 1), (1, -1), (-1, 1), (-1, -1), (2, 0), (-2, 0)]
SLOT = {peer: k for k, peer in enumerate(PEERS)}


def split_table(table):
    high = table.astype(jnp.bfloat16)
    low = (table - high.astype(np.float64)).astype(jnp.bfloat16)
    return high, low


def make_tables():
    index = np.arange(SIZE)
    angles = (index[:, None] * index[None, :] % SIZE) * (2.0 * math.pi / SIZE)
    cosines, sines = np.cos(angles), np.sin(angles)
    sign = np.where(index % 2 == 0, 1.0, -1.0)
    real = cosines[:, :HALF]
    imag = -sines[:, :HALF].copy()
    imag[:, 0] = sign
    zero = np.zeros((SIZE, HALF))
    along_x = np.block([[real, zero, imag, zero], [zero, real, zero, imag]])
    along_u = np.block([[cosines, -sines], [sines, cosines]])
    back_real = 2.0 * cosines[:HALF]
    back_real[0] = 1.0
    back_imag = -2.0 * sines[:HALF]
    back_imag[0] = sign
    wide = np.zeros((HALF, SIZE))
    along_v = np.block(
        [[back_real, wide], [wide, back_real], [back_imag, wide], [wide, back_imag]]
    )
    parts = []
    for table in (along_x, along_u, along_v):
        parts.extend(split_table(table))
    return np.stack(parts)


def fit_even(function, terms):
    nodes = 0.25 * (0.5 + 0.5 * np.cos(np.pi * (np.arange(200) + 0.5) / 200))
    powers = np.vander(nodes * 4.0, terms, increasing=True)
    solved = np.linalg.lstsq(powers, function(np.sqrt(nodes)), rcond=None)[0]
    return [float(c) for c in solved * 4.0 ** np.arange(terms)]


SIN_FIT = fit_even(lambda r: np.sin(np.pi * r) / r, 6)
COS_FIT = fit_even(lambda r: np.cos(np.pi * r), 7)


def horner(coefficients, value):
    total = coefficients[-1]
    for c in coefficients[-2::-1]:
        total = total * value + c
    return total


def turn(turns):
    r = turns - jnp.round(turns)
    squared = r * r
    s = r * horner(SIN_FIT, squared)
    c = horner(COS_FIT, squared)
    return 1.0 - 2.0 * s * s, 2.0 * s * c


def halves(values):
    high = values.astype(BF16)
    return high, (values - high.astype(F32)).astype(BF16)


def dot(a, b):
    return jnp.dot(a, b, preferred_element_type=F32)


def left_product(table, values):
    high, low = halves(values)
    return dot(table[0], high) + (dot(table[0], low) + dot(table[1], high))


def right_product(values, table):
    high, low = halves(values)
    return dot(high, table[0]) + (dot(low, table[0]) + dot(high, table[1]))


def iota(shape, dim):
    return lax.broadcasted_iota(jnp.int32, shape, dim)


def spectrum(image, along_x, along_u):
    rows = jnp.concatenate([image[:, :256], image[:, 256:]], axis=0)
    first = dot(rows, along_x[0]) + dot(rows, along_x[1])
    real = jnp.concatenate([first[:SIZE, :SIZE], first[SIZE:, :SIZE]], axis=1)
    imag = jnp.concatenate([first[:SIZE, SIZE:], first[SIZE:, SIZE:]], axis=1)
    edge = iota((SIZE, 256), 1) % HALF == 0
    main = jnp.concatenate([real, jnp.where(edge, 0.0, -imag)], axis=0)
    last = jnp.where(edge, imag, 0.0)
    full = left_product(along_u, main)
    nyquist = left_product((along_u[0][:, :SIZE], along_u[1][:, :SIZE]), last)
    constant = edge & (iota((SIZE, 256), 0) == 0)
    full_real = jnp.where(constant, 0.0, full[:SIZE])
    full_imag = jnp.where(constant, 0.0, full[SIZE:])
    return full_real, full_imag, nyquist[:SIZE], nyquist[SIZE:]


def column_sums(values):
    middle = values[HALF : HALF + 1]
    return jnp.sum(values, axis=0, keepdims=True) - middle, middle


def energy_rows(spec):
    real, imag, edge_real, edge_imag = spec
    weight = jnp.where(iota((SIZE, 256), 1) % HALF == 0, 1.0, 2.0)
    rows = iota((SIZE, 256), 0)
    out = []
    for power in (weight * (real * real + imag * imag), edge_real * edge_real + edge_imag * edge_imag):
        out.append(jnp.sum(jnp.where(rows == HALF, 0.0, power), axis=0, keepdims=True))
        out.append(power[HALF : HALF + 1])
    return out


def to_lanes(rows):
    lane = iota((rows.shape[0], SIZE), 1)
    left, right = rows[:, :SIZE], rows[:, SIZE:]
    total = jnp.zeros((rows.shape[0], SIZE), F32)
    for c, (part, low) in enumerate([(left, True), (left, False), (right, True), (right, False)]):
        kept = jnp.where((lane < HALF) == low, part, 0.0)
        total = total + jnp.where(lane == c, jnp.sum(kept, axis=1, keepdims=True), 0.0)
    return total


def from_lanes(rows):
    shape = (rows.shape[0], SIZE)
    lane = iota(shape, 1)
    spread = [jnp.broadcast_to(rows[:, c : c + 1], shape) for c in range(4)]
    return jnp.concatenate(
        [
            jnp.where(lane < HALF, spread[0], spread[1]),
            jnp.where(lane < HALF, spread[2], spread[3]),
        ],
        axis=1,
    )


def stack(rows):
    width = rows[0].shape[1]
    pad = -len(rows) % 8
    return jnp.concatenate(rows + [jnp.zeros((1, width), F32)] * pad, axis=0)


def prepare(own, other):
    ar, ai, aer, aei = own
    br, bi, ber, bei = other
    cross_real = ar * br + ai * bi
    cross_imag = ar * bi - ai * br
    edge_real = aer * ber + aei * bei
    edge_imag = aer * bei - aei * ber
    rows = energy_rows(own) + energy_rows(other)
    rows = [row * (1.0 / (SIZE * SIZE)) for row in rows] + [edge_real[HALF : HALF + 1]]
    return cross_real - edge_imag, cross_imag + edge_real, to_lanes(stack(rows))


def sums_of_lags(field_own, field_other, cross_real, cross_imag, terms, along_u, along_v):
    dy_own, dy_other = field_own, field_other
    dx_own = pltpu.roll(field_own, SIZE - 4, 1)
    dx_other = pltpu.roll(field_other, SIZE - 4, 1)
    cosines, _ = turn(
        0.5 * stack([dy_own, dx_own, dy_own + dx_own, dy_other, dx_other, dy_other + dx_other])
    )
    squares = cosines * cosines
    energy_own = terms[0:1] + squares[0:1] * terms[1:2] + squares[1:2] * terms[2:3] + squares[2:3] * terms[3:4]
    energy_other = terms[4:5] + squares[3:4] * terms[5:6] + squares[4:5] * terms[6:7] + squares[5:6] * terms[7:8]
    scale = (SHARP / (SIZE * SIZE)) / jnp.sqrt(energy_own * energy_other + EPS)
    factor_y = cosines[0:1] * cosines[3:4]
    factor_x = cosines[1:2] * cosines[4:5]
    corner = (cosines[2:3] * cosines[5:6] - factor_y * factor_x) * terms[8:9]
    spread = from_lanes(
        stack(
            [
                (dy_own - dy_other) * (-1.0 / SIZE),
                (dx_own - dx_other) * (-1.0 / SIZE),
                factor_y,
                factor_x * scale,
                scale,
                corner * scale,
            ]
        )
    )
    u = iota((SIZE, 256), 0)
    signed_u = jnp.where(u >= HALF, u - SIZE, u).astype(F32)
    turn_cos, turn_sin = turn(signed_u * spread[0:1])
    turn_cos = jnp.where(u == HALF, spread[2:3], turn_cos)
    turn_sin = jnp.where(u == HALF, 0.0, turn_sin)
    shifted = jnp.concatenate(
        [
            cross_real * turn_cos - cross_imag * turn_sin,
            cross_real * turn_sin + cross_imag * turn_cos,
        ],
        axis=0,
    )
    columns = left_product(along_u, shifted)
    real, imag = columns[:SIZE], columns[SIZE:]
    v = iota((1, 256), 1) % HALF
    row_cos, row_sin = turn(v.astype(F32) * spread[1:2])
    row_cos = row_cos * spread[4:5]
    row_sin = row_sin * spread[4:5]
    row_cos_edge = jnp.where(v == 0, spread[3:4], row_cos)
    sign = (1 - 2 * (u % 2)).astype(F32)
    moved_real = real * row_cos - imag * row_sin
    moved_imag = real * row_sin + imag * row_cos_edge + sign * jnp.where(v == 0, spread[5:6], 0.0)
    pairs = jnp.concatenate(
        [
            jnp.concatenate([moved_real[:, :SIZE], moved_imag[:, :SIZE]], axis=1),
            jnp.concatenate([moved_real[:, SIZE:], moved_imag[:, SIZE:]], axis=1),
        ],
        axis=0,
    )
    weights = jnp.exp(right_product(pairs, along_v))

    b = iota((1, 256), 1) % SIZE
    signed_b = jnp.where(b >= HALF, b - SIZE, b).astype(F32)
    totals, moments_a, moments_b, ends_a, ends_b = [], [], [], [], []
    for g in range(2):
        block = weights[g * SIZE : (g + 1) * SIZE]
        total = jnp.sum(block, axis=0, keepdims=True)
        totals.append(total)
        moments_a.append(jnp.sum(block * signed_u, axis=0, keepdims=True))
        moments_b.append(total * signed_b)
        ends_a.append(block[HALF : HALF + 1])
        ends_b.append(jnp.where(b == HALF, total, 0.0))
    rows = stack(totals + moments_a + moments_b + ends_a + ends_b)
    k = iota((16, SIZE), 0)
    lane = iota((16, SIZE), 1)
    kind, g = k // 2, k % 2
    out = [0.0, 0.0, 0.0]
    for which in range(2):
        reduced = jnp.sum(rows[:, which * SIZE : (which + 1) * SIZE], axis=1, keepdims=True)
        here = (lane % 4 == 2 * g + which) & (lane < 8)
        component = lane // 4
        for n, chosen in enumerate(
            (kind == 0, kind == 1 + component, kind == 3 + component)
        ):
            out[n] = out[n] + jnp.sum(jnp.where(here & chosen, reduced, 0.0), axis=0, keepdims=True)
    return out


def kernel(
    images, displacement, fold_mask, tables, relaxed_ref, mean_ref,
    own_image, other_image, table, disp, mask, first, first_in, sent, received,
    load_sem, image_send, image_recv, first_send, first_recv, send_sem, recv_sem,
):
    section, row = lax.axis_index("sec"), lax.axis_index("row")
    sections, nrows = lax.axis_size("sec"), lax.axis_size("row")

    def device(peer):
        return (lax.rem(section + peer[0] + sections, sections), row + peer[1])

    def when_there(peer, action):
        if peer[1] == 0:
            action()
        else:
            pl.when((row + peer[1] >= 0) & (row + peer[1] < nrows))(action)

    barrier = pltpu.get_barrier_semaphore()
    for peer in PEERS:
        when_there(
            peer,
            lambda peer=peer: pl.semaphore_signal(
                barrier, inc=1, device_id=device(peer), device_id_type=COORD
            ),
        )
    loads = [
        pltpu.make_async_copy(displacement, disp, load_sem.at[0]),
        pltpu.make_async_copy(fold_mask, mask, load_sem.at[1]),
        pltpu.make_async_copy(images, own_image, load_sem.at[2]),
        pltpu.make_async_copy(tables, table, load_sem.at[3]),
    ]
    for load in loads:
        load.start()
    loads[0].wait()
    loads[1].wait()
    first[...] = jnp.zeros((1, SIZE), F32)
    for k in range(2):
        first[:, 4 * k : 4 * k + 4] = disp[k, 0]
        first[:, 8 + 4 * k : 12 + 4 * k] = mask[k, 0].astype(F32)

    inside = (row > 0).astype(jnp.int32) + (row < nrows - 1).astype(jnp.int32)
    pl.semaphore_wait(barrier, 4 + 3 * inside)

    image_copies, first_copies = [], []
    for k, peer in enumerate(NEAR):
        part = pl.ds(256 * (1 - k), 256)
        image_copies.append(
            pltpu.make_async_remote_copy(
                src_ref=images.at[:, part],
                dst_ref=other_image.at[:, part],
                send_sem=image_send.at[k],
                recv_sem=image_recv.at[1 - k],
                device_id=device(peer),
                device_id_type=COORD,
            )
        )
        first_copies.append(
            pltpu.make_async_remote_copy(
                src_ref=first,
                dst_ref=first_in.at[k],
                send_sem=first_send.at[k],
                recv_sem=first_recv.at[k],
                device_id=device(peer),
                device_id_type=COORD,
            )
        )
    for copy in image_copies + first_copies:
        copy.start()

    loads[2].wait()
    loads[3].wait()
    along_x, along_u, along_v = (
        (table[0], table[1]), (table[2], table[3]), (table[4], table[5])
    )
    own_spectrum = spectrum(own_image[...], along_x, along_u)

    for copy in first_copies:
        copy.wait_recv()
    lane = iota((1, SIZE), 1)
    column = lane % 4
    low = column < 2
    below, above, mine = first_in[0], first_in[1], first[...]

    def weights(values, position):
        aligned = pltpu.roll(values, SIZE - 8, 1)
        both = aligned * jnp.where(
            lane < 4, (position > 0).astype(F32), (position < sections - 1).astype(F32)
        )
        both = jnp.where(lane < 8, both, 0.0)
        lower = jnp.where(lane < 4, both, pltpu.roll(both, 4, 1))
        upper = jnp.where(lane < 4, pltpu.roll(both, SIZE - 4, 1), both)
        norm = 1.0 / jnp.maximum(lower + upper, 1.0)
        return jnp.where(lane < 8, lower * norm, 0.0), jnp.where(lane < 8, upper * norm, 0.0)

    lower_mine, upper_mine = weights(mine, section)
    lower_above, _ = weights(above, lax.rem(section + 1, sections))
    _, upper_below = weights(below, lax.rem(section + sections - 1, sections))
    coef_own = jnp.where(low, upper_mine, lower_mine)
    coef_other = jnp.where(low, lower_above, upper_below)
    field = jnp.where(lane < 8, mine, 0.0)
    field_other = jnp.where(lane < 8, jnp.where(low, above, below), 0.0)

    for copy in image_copies:
        copy.wait_recv()
    other_spectrum = spectrum(other_image[...], along_x, along_u)
    cross_real, cross_imag, terms = prepare(own_spectrum, other_spectrum)

    def left_of(values):
        return pltpu.roll(values, 1, 1)

    def right_of(values):
        return pltpu.roll(values, SIZE - 1, 1)

    copies = []
    for step in range(ITERS):
        last = step == ITERS - 1
        total, moment, end = sums_of_lags(
            field, field_other, cross_real, cross_imag, terms, along_u, along_v
        )
        total = jnp.where(lane < 8, total, 1.0)
        offset = moment / total
        mirrored = -offset - SIZE * (end / total)
        mean_own = coef_own * offset
        share = STEP * coef_other * mirrored
        sent[step, 0] = field + STEP * mean_own
        sent[step, 1] = share
        peers = [peer for peer in PEERS if abs(peer[0]) < 2] if last else PEERS

        def exchange(peer):
            return pltpu.make_async_remote_copy(
                src_ref=sent.at[step],
                dst_ref=received.at[step, SLOT[peer]],
                send_sem=send_sem.at[step, SLOT[peer]],
                recv_sem=recv_sem.at[step, SLOT[peer]],
                device_id=device(peer),
                device_id_type=COORD,
            )

        for peer in peers:
            when_there(peer, lambda peer=peer: exchange(peer).start())
        for peer in peers:
            opposite = (-peer[0], -peer[1])
            when_there(opposite, lambda peer=peer: exchange(peer).wait_recv())

        def base(ds, dr):
            if (ds, dr) == (0, 0):
                return sent[step, 0]
            return received[step, SLOT[(-ds, -dr)], 0]

        def shared(ds, dr):
            if (ds, dr) == (0, 0):
                return sent[step, 1]
            return received[step, SLOT[(-ds, -dr)], 1]

        there = {-1: row > 0, 1: row < nrows - 1}
        own_rows = {
            dr: base(0, dr) + jnp.where(low, shared(-1, dr), shared(1, dr)) for dr in (-1, 0, 1)
        }
        mine = own_rows[0]
        around = (
            jnp.where(there[-1], own_rows[-1], 0.0)
            + jnp.where(there[1], own_rows[1], 0.0)
            + jnp.where(column == 0, 0.0, left_of(mine))
            + jnp.where(column == 3, 0.0, right_of(mine))
        )
        smoothed = mine + STIFF * (around - 4.0 * mine)
        if last:
            mean = mean_own + (1.0 / STEP) * jnp.where(low, shared(-1, 0), shared(1, 0))
            for k in range(2):
                relaxed_ref[k, 0] = smoothed[:, 4 * k : 4 * k + 4]
                mean_ref[k, 0] = mean[:, 4 * k : 4 * k + 4]
        else:
            other_rows = {
                dr: jnp.where(low, base(1, dr), base(-1, dr)) + shared(0, dr) for dr in (-1, 0, 1)
            }
            across = jnp.where(
                column == 1, base(-1, 0) + shared(-2, 0), base(1, 0) + shared(2, 0)
            )
            them = other_rows[0]
            around = (
                jnp.where(there[-1], other_rows[-1], 0.0)
                + jnp.where(there[1], other_rows[1], 0.0)
                + jnp.where(
                    column == 0, 0.0, jnp.where(column == 2, left_of(across), left_of(them))
                )
                + jnp.where(
                    column == 3, 0.0, jnp.where(column == 1, right_of(across), right_of(them))
                )
            )
            field = jnp.where(lane < 8, smoothed, 0.0)
            field_other = jnp.where(lane < 8, them + STIFF * (around - 4.0 * them), 0.0)

    for copy in image_copies + first_copies:
        copy.wait_send()
    for step in range(ITERS):
        for peer in PEERS:
            if step == ITERS - 1 and abs(peer[0]) == 2:
                continue
            when_there(
                peer,
                lambda peer=peer, step=step: pltpu.make_async_remote_copy(
                    src_ref=sent.at[step],
                    dst_ref=received.at[step, SLOT[peer]],
                    send_sem=send_sem.at[step, SLOT[peer]],
                    recv_sem=recv_sem.at[step, SLOT[peer]],
                    device_id=device(peer),
                    device_id_type=COORD,
                ).wait_send(),
            )


def per_device(section_images, displacement, fold_mask):
    tables = jnp.asarray(make_tables())
    result = jax.ShapeDtypeStruct((2, 1, 1, 4), F32)
    return pl.pallas_call(
        kernel,
        out_shape=(result, result),
        in_specs=[pl.BlockSpec(memory_space=pl.ANY)] * 4,
        out_specs=[pl.BlockSpec(memory_space=pltpu.VMEM)] * 2,
        scratch_shapes=[
            pltpu.VMEM((SIZE, 512), BF16),
            pltpu.VMEM((SIZE, 512), BF16),
            pltpu.VMEM((6, 256, 256), BF16),
            pltpu.VMEM((2, 1, 1, 4), F32),
            pltpu.VMEM((2, 1, 1, 4), jnp.int32),
            pltpu.VMEM((1, SIZE), F32),
            pltpu.VMEM((2, 1, SIZE), F32),
            pltpu.VMEM((ITERS, 2, 1, SIZE), F32),
            pltpu.VMEM((ITERS, len(PEERS), 2, 1, SIZE), F32),
            pltpu.SemaphoreType.DMA((4,)),
            pltpu.SemaphoreType.DMA((2,)),
            pltpu.SemaphoreType.DMA((2,)),
            pltpu.SemaphoreType.DMA((2,)),
            pltpu.SemaphoreType.DMA((2,)),
            pltpu.SemaphoreType.DMA((ITERS, len(PEERS))),
            pltpu.SemaphoreType.DMA((ITERS, len(PEERS))),
        ],
        compiler_params=pltpu.CompilerParams(
            collective_id=0, has_side_effects=True, vmem_limit_bytes=32 * 1024 * 1024
        ),
    )(section_images[0], displacement, fold_mask, tables)


def solution(mesh):
    in_specs = (P("sec", "row", None), P(None, "sec", "row", None), P(None, "sec", "row", None))
    out_specs = (P(None, "sec", "row", None), P(None, "sec", "row", None))
    return jax.shard_map(
        per_device, mesh=mesh, in_specs=in_specs, out_specs=out_specs, check_vma=False
    )
```

```python
import functools
import math

import jax
import jax.numpy as jnp
import numpy as np
from jax import lax
from jax.experimental import pallas as pl
from jax.experimental.pallas import tpu as pltpu
from jax.sharding import PartitionSpec as P

SIZE = 128
HALF = 64
ITERS = 3
STEP = 0.5
STIFF = 0.2
EPS = 1e-6
SHARP = 0.5 * SIZE
F32 = jnp.float32
BF16 = jnp.bfloat16
COORD = pl.DeviceIdType.MESH

PEERS = [(1, 0), (-1, 0), (0, 1), (0, -1), (1, 1), (1, -1), (-1, 1), (-1, -1)]
LAST_PEERS = [(-1, 0), (0, 1), (0, -1), (-1, 1), (-1, -1)]
SLOT = {peer: k for k, peer in enumerate(PEERS)}


def split_table(table):
    high = table.astype(jnp.bfloat16)
    low = (table - high.astype(np.float64)).astype(jnp.bfloat16)
    return high, low


def make_tables():
    index = np.arange(SIZE)
    angles = (index[:, None] * index[None, :] % SIZE) * (2.0 * math.pi / SIZE)
    cosines, sines = np.cos(angles), np.sin(angles)
    sign = np.where(index % 2 == 0, 1.0, -1.0)
    real = cosines[:, :HALF]
    imag = -sines[:, :HALF].copy()
    imag[:, 0] = sign
    zero = np.zeros((SIZE, HALF))
    along_x = np.block([[real, zero, imag, zero], [zero, real, zero, imag]])
    along_u = np.block([[cosines, -sines], [sines, cosines]])
    back_real = 2.0 * cosines[:HALF]
    back_real[0] = 1.0
    back_imag = -2.0 * sines[:HALF]
    back_imag[0] = sign
    wide = np.zeros((HALF, SIZE))
    along_v = np.block(
        [[back_real, wide], [wide, back_real], [back_imag, wide], [wide, back_imag]]
    )
    parts = []
    for table in (along_x, along_u, along_v):
        parts.extend(split_table(table))
    return np.stack(parts)


def fit_even(function, terms):
    nodes = 0.25 * (0.5 + 0.5 * np.cos(np.pi * (np.arange(200) + 0.5) / 200))
    powers = np.vander(nodes * 4.0, terms, increasing=True)
    solved = np.linalg.lstsq(powers, function(np.sqrt(nodes)), rcond=None)[0]
    return [float(c) for c in solved * 4.0 ** np.arange(terms)]


SIN_FIT = fit_even(lambda r: np.sin(np.pi * r) / r, 6)
COS_FIT = fit_even(lambda r: np.cos(np.pi * r), 7)


def horner(coefficients, value):
    total = coefficients[-1]
    for c in coefficients[-2::-1]:
        total = total * value + c
    return total


def turn(turns):
    r = turns - jnp.round(turns)
    squared = r * r
    s = r * horner(SIN_FIT, squared)
    c = horner(COS_FIT, squared)
    return 1.0 - 2.0 * s * s, 2.0 * s * c


def halves(values):
    high = values.astype(BF16)
    return high, (values - high.astype(F32)).astype(BF16)


def dot(a, b):
    return jnp.dot(a, b, preferred_element_type=F32)


def left_product(table, values):
    high, low = halves(values)
    return dot(table[0], high) + (dot(table[0], low) + dot(table[1], high))


def right_product(values, table):
    high, low = halves(values)
    return dot(high, table[0]) + (dot(low, table[0]) + dot(high, table[1]))


def iota(shape, dim):
    return lax.broadcasted_iota(jnp.int32, shape, dim)


def spectrum(image, along_x, along_u):
    rows = jnp.concatenate([image[:, :256], image[:, 256:]], axis=0)
    first = dot(rows, along_x[0]) + dot(rows, along_x[1])
    real = jnp.concatenate([first[:SIZE, :SIZE], first[SIZE:, :SIZE]], axis=1)
    imag = jnp.concatenate([first[:SIZE, SIZE:], first[SIZE:, SIZE:]], axis=1)
    edge = iota((SIZE, 256), 1) % HALF == 0
    main = jnp.concatenate([real, jnp.where(edge, 0.0, -imag)], axis=0)
    last = jnp.where(edge, imag, 0.0)
    full = left_product(along_u, main)
    nyquist = left_product((along_u[0][:, :SIZE], along_u[1][:, :SIZE]), last)
    constant = edge & (iota((SIZE, 256), 0) == 0)
    full_real = jnp.where(constant, 0.0, full[:SIZE])
    full_imag = jnp.where(constant, 0.0, full[SIZE:])
    return full_real, full_imag, nyquist[:SIZE], nyquist[SIZE:]


def column_sums(values):
    middle = values[HALF : HALF + 1]
    return jnp.sum(values, axis=0, keepdims=True) - middle, middle


def energy_rows(spec):
    real, imag, edge_real, edge_imag = spec
    weight = jnp.where(iota((SIZE, 256), 1) % HALF == 0, 1.0, 2.0)
    rows = iota((SIZE, 256), 0)
    out = []
    for power in (weight * (real * real + imag * imag), edge_real * edge_real + edge_imag * edge_imag):
        out.append(jnp.sum(jnp.where(rows == HALF, 0.0, power), axis=0, keepdims=True))
        out.append(power[HALF : HALF + 1])
    return out


def to_lanes(rows):
    lane = iota((rows.shape[0], SIZE), 1)
    left, right = rows[:, :SIZE], rows[:, SIZE:]
    total = jnp.zeros((rows.shape[0], SIZE), F32)
    for c, (part, low) in enumerate([(left, True), (left, False), (right, True), (right, False)]):
        kept = jnp.where((lane < HALF) == low, part, 0.0)
        total = total + jnp.where(lane == c, jnp.sum(kept, axis=1, keepdims=True), 0.0)
    return total


def from_lanes(rows):
    shape = (rows.shape[0], SIZE)
    lane = iota(shape, 1)
    spread = [jnp.broadcast_to(rows[:, c : c + 1], shape) for c in range(4)]
    return jnp.concatenate(
        [
            jnp.where(lane < HALF, spread[0], spread[1]),
            jnp.where(lane < HALF, spread[2], spread[3]),
        ],
        axis=1,
    )


def stack(rows):
    width = rows[0].shape[1]
    pad = -len(rows) % 8
    return jnp.concatenate(rows + [jnp.zeros((1, width), F32)] * pad, axis=0)


def prepare(own, other):
    ar, ai, aer, aei = own
    br, bi, ber, bei = other
    cross_real = ar * br + ai * bi
    cross_imag = ar * bi - ai * br
    edge_real = aer * ber + aei * bei
    edge_imag = aer * bei - aei * ber
    rows = energy_rows(own) + energy_rows(other)
    rows = [row * (1.0 / (SIZE * SIZE)) for row in rows] + [edge_real[HALF : HALF + 1]]
    return cross_real - edge_imag, cross_imag + edge_real, to_lanes(stack(rows))


def sums_of_lags(field_own, field_other, cross_real, cross_imag, terms, along_u, along_v):
    dy_own, dy_other = field_own, field_other
    dx_own = pltpu.roll(field_own, SIZE - 4, 1)
    dx_other = pltpu.roll(field_other, SIZE - 4, 1)
    cosines, _ = turn(
        0.5 * stack([dy_own, dx_own, dy_own + dx_own, dy_other, dx_other, dy_other + dx_other])
    )
    squares = cosines * cosines
    energy_own = terms[0:1] + squares[0:1] * terms[1:2] + squares[1:2] * terms[2:3] + squares[2:3] * terms[3:4]
    energy_other = terms[4:5] + squares[3:4] * terms[5:6] + squares[4:5] * terms[6:7] + squares[5:6] * terms[7:8]
    scale = (SHARP / (SIZE * SIZE)) / jnp.sqrt(energy_own * energy_other + EPS)
    factor_y = cosines[0:1] * cosines[3:4]
    factor_x = cosines[1:2] * cosines[4:5]
    corner = (cosines[2:3] * cosines[5:6] - factor_y * factor_x) * terms[8:9]
    spread = from_lanes(
        stack(
            [
                (dy_own - dy_other) * (-1.0 / SIZE),
                (dx_own - dx_other) * (-1.0 / SIZE),
                factor_y,
                factor_x * scale,
                scale,
                corner * scale,
            ]
        )
    )
    u = iota((SIZE, 256), 0)
    signed_u = jnp.where(u >= HALF, u - SIZE, u).astype(F32)
    turn_cos, turn_sin = turn(signed_u * spread[0:1])
    turn_cos = jnp.where(u == HALF, spread[2:3], turn_cos)
    turn_sin = jnp.where(u == HALF, 0.0, turn_sin)
    shifted = jnp.concatenate(
        [
            cross_real * turn_cos - cross_imag * turn_sin,
            cross_real * turn_sin + cross_imag * turn_cos,
        ],
        axis=0,
    )
    columns = left_product(along_u, shifted)
    real, imag = columns[:SIZE], columns[SIZE:]
    v = iota((1, 256), 1) % HALF
    row_cos, row_sin = turn(v.astype(F32) * spread[1:2])
    row_cos = row_cos * spread[4:5]
    row_sin = row_sin * spread[4:5]
    row_cos_edge = jnp.where(v == 0, spread[3:4], row_cos)
    sign = (1 - 2 * (u % 2)).astype(F32)
    moved_real = real * row_cos - imag * row_sin
    moved_imag = real * row_sin + imag * row_cos_edge + sign * jnp.where(v == 0, spread[5:6], 0.0)
    pairs = jnp.concatenate(
        [
            jnp.concatenate([moved_real[:, :SIZE], moved_imag[:, :SIZE]], axis=1),
            jnp.concatenate([moved_real[:, SIZE:], moved_imag[:, SIZE:]], axis=1),
        ],
        axis=0,
    )
    weights = jnp.exp(right_product(pairs, along_v))

    b = iota((1, 256), 1) % SIZE
    signed_b = jnp.where(b >= HALF, b - SIZE, b).astype(F32)
    totals, moments_a, moments_b, ends_a, ends_b = [], [], [], [], []
    for g in range(2):
        block = weights[g * SIZE : (g + 1) * SIZE]
        total = jnp.sum(block, axis=0, keepdims=True)
        totals.append(total)
        moments_a.append(jnp.sum(block * signed_u, axis=0, keepdims=True))
        moments_b.append(total * signed_b)
        ends_a.append(block[HALF : HALF + 1])
        ends_b.append(jnp.where(b == HALF, total, 0.0))
    rows = stack(totals + moments_a + moments_b + ends_a + ends_b)
    k = iota((16, SIZE), 0)
    lane = iota((16, SIZE), 1)
    kind, g = k // 2, k % 2
    out = [0.0, 0.0, 0.0]
    for which in range(2):
        reduced = jnp.sum(rows[:, which * SIZE : (which + 1) * SIZE], axis=1, keepdims=True)
        here = (lane % 4 == 2 * g + which) & (lane < 8)
        component = lane // 4
        for n, chosen in enumerate(
            (kind == 0, kind == 1 + component, kind == 3 + component)
        ):
            out[n] = out[n] + jnp.sum(jnp.where(here & chosen, reduced, 0.0), axis=0, keepdims=True)
    return out


def kernel(
    images, displacement, fold_mask, tables, result_ref,
    own_image, other_image, table, disp, mask, first, first_in, sent, received,
    load_sem, image_sem, first_sem, send_sem, recv_sem,
):
    section, row = lax.axis_index("sec"), lax.axis_index("row")
    sections, nrows = lax.axis_size("sec"), lax.axis_size("row")
    above, below = section < sections - 1, section > 0
    there = {-1: row > 0, 1: row < nrows - 1}

    def device(peer):
        return (section + peer[0], row + peer[1])

    def when_there(peer, action):
        conditions = []
        if peer[0] != 0:
            conditions.append(above if peer[0] > 0 else below)
        if peer[1] != 0:
            conditions.append(there[peer[1]])
        pl.when(functools.reduce(jnp.logical_and, conditions))(action)

    barrier = pltpu.get_barrier_semaphore()
    for peer in PEERS:
        when_there(
            peer,
            lambda peer=peer: pl.semaphore_signal(
                barrier, inc=1, device_id=device(peer), device_id_type=COORD
            ),
        )
    loads = [
        pltpu.make_async_copy(displacement, disp, load_sem.at[0]),
        pltpu.make_async_copy(fold_mask, mask, load_sem.at[1]),
        pltpu.make_async_copy(images, own_image, load_sem.at[2]),
        pltpu.make_async_copy(tables, table, load_sem.at[3]),
    ]
    for load in loads:
        load.start()
    loads[0].wait()
    loads[1].wait()
    first[...] = jnp.zeros((1, SIZE), F32)
    for k in range(2):
        first[:, 4 * k : 4 * k + 4] = disp[k, 0]
        first[:, 8 + 4 * k : 12 + 4 * k] = mask[k, 0].astype(F32)

    def count(flag):
        return flag.astype(jnp.int32)

    along = count(above) + count(below)
    beside = count(there[-1]) + count(there[1])
    pl.semaphore_wait(barrier, along + beside + along * beside)

    first_copy = pltpu.make_async_remote_copy(
        src_ref=first,
        dst_ref=first_in,
        send_sem=first_sem.at[0],
        recv_sem=first_sem.at[1],
        device_id=device((1, 0)),
        device_id_type=COORD,
    )
    image_copy = pltpu.make_async_remote_copy(
        src_ref=images,
        dst_ref=other_image,
        send_sem=image_sem.at[0],
        recv_sem=image_sem.at[1],
        device_id=device((1, 0)),
        device_id_type=COORD,
    )

    @pl.when(above)
    def _():
        first_copy.start()
        image_copy.start()

    loads[2].wait()
    loads[3].wait()
    along_x, along_u, along_v = (
        (table[0], table[1]), (table[2], table[3]), (table[4], table[5])
    )
    own_spectrum = spectrum(own_image[...], along_x, along_u)

    lane = iota((1, SIZE), 1)
    column = lane % 4

    @pl.when(below)
    def _():
        first_copy.wait_recv()

    @pl.when(jnp.logical_not(below))
    def _():
        first_in[...] = jnp.zeros((1, SIZE), F32)
        other_image[...] = jnp.zeros((SIZE, 512), BF16)

    mine, under = first[...], first_in[...]

    def weights(values, position):
        aligned = pltpu.roll(values, SIZE - 8, 1)
        both = aligned * jnp.where(
            lane < 4, (position > 0).astype(F32), (position < sections - 1).astype(F32)
        )
        both = jnp.where(lane < 8, both, 0.0)
        lower = jnp.where(lane < 4, both, pltpu.roll(both, 4, 1))
        upper = jnp.where(lane < 4, pltpu.roll(both, SIZE - 4, 1), both)
        norm = 1.0 / jnp.maximum(lower + upper, 1.0)
        return jnp.where(lane < 8, lower * norm, 0.0), jnp.where(lane < 8, upper * norm, 0.0)

    coef_own, _ = weights(mine, section)
    _, coef_other = weights(under, section - 1)
    field = jnp.where(lane < 8, mine, 0.0)
    field_other = jnp.where(lane < 8, under, 0.0)

    @pl.when(below)
    def _():
        image_copy.wait_recv()

    other_spectrum = spectrum(other_image[...], along_x, along_u)
    cross_real, cross_imag, terms = prepare(own_spectrum, other_spectrum)

    def smooth(rows):
        current = rows[0]
        around = (
            jnp.where(there[-1], rows[-1], 0.0)
            + jnp.where(there[1], rows[1], 0.0)
            + jnp.where(column == 0, 0.0, pltpu.roll(current, 1, 1))
            + jnp.where(column == 3, 0.0, pltpu.roll(current, SIZE - 1, 1))
        )
        return current + STIFF * (around - 4.0 * current)

    def exchange(step, peer):
        return pltpu.make_async_remote_copy(
            src_ref=sent.at[step],
            dst_ref=received.at[step, SLOT[peer]],
            send_sem=send_sem.at[step, SLOT[peer]],
            recv_sem=recv_sem.at[step, SLOT[peer]],
            device_id=device(peer),
            device_id_type=COORD,
        )

    for step in range(ITERS):
        last = step == ITERS - 1
        total, moment, end = sums_of_lags(
            field, field_other, cross_real, cross_imag, terms, along_u, along_v
        )
        total = jnp.where(lane < 8, total, 1.0)
        offset = moment / total
        mirrored = -offset - SIZE * (end / total)
        mean_own = coef_own * offset
        sent[step, 0] = field + STEP * mean_own
        sent[step, 1] = STEP * coef_other * mirrored
        peers = LAST_PEERS if last else PEERS
        for peer in peers:
            when_there(peer, lambda peer=peer: exchange(step, peer).start())
        for peer in peers:
            when_there(
                (-peer[0], -peer[1]), lambda peer=peer: exchange(step, peer).wait_recv()
            )

        def part(kind, ds, dr):
            if (ds, dr) == (0, 0):
                return sent[step, kind]
            return received[step, SLOT[(-ds, -dr)], kind]

        shared = {dr: jnp.where(above, part(1, 1, dr), 0.0) for dr in (-1, 0, 1)}
        smoothed = smooth({dr: part(0, 0, dr) + shared[dr] for dr in (-1, 0, 1)})
        if last:
            mean = mean_own + (1.0 / STEP) * shared[0]
            for k in range(2):
                result_ref[k, 0] = smoothed[:, 4 * k : 4 * k + 4]
                result_ref[2 + k, 0] = mean[:, 4 * k : 4 * k + 4]
        else:
            smoothed_other = smooth({dr: part(0, -1, dr) + part(1, 0, dr) for dr in (-1, 0, 1)})
            field = jnp.where(lane < 8, smoothed, 0.0)
            field_other = jnp.where((lane < 8) & below, smoothed_other, 0.0)

    @pl.when(above)
    def _():
        first_copy.wait_send()
        image_copy.wait_send()

    for step in range(ITERS):
        for peer in LAST_PEERS if step == ITERS - 1 else PEERS:
            when_there(peer, lambda peer=peer, step=step: exchange(step, peer).wait_send())


def per_device(section_images, displacement, fold_mask):
    tables = jnp.asarray(make_tables())
    result = jax.ShapeDtypeStruct((4, 1, 1, 4), F32)
    both = pl.pallas_call(
        kernel,
        out_shape=result,
        in_specs=[pl.BlockSpec(memory_space=pltpu.HBM)] * 4,
        out_specs=pl.BlockSpec(memory_space=pltpu.VMEM),
        scratch_shapes=[
            pltpu.VMEM((SIZE, 512), BF16),
            pltpu.VMEM((SIZE, 512), BF16),
            pltpu.VMEM((6, 256, 256), BF16),
            pltpu.VMEM((2, 1, 1, 4), F32),
            pltpu.VMEM((2, 1, 1, 4), jnp.int32),
            pltpu.VMEM((1, SIZE), F32),
            pltpu.VMEM((1, SIZE), F32),
            pltpu.VMEM((ITERS, 2, 1, SIZE), F32),
            pltpu.VMEM((ITERS, len(PEERS), 2, 1, SIZE), F32),
            pltpu.SemaphoreType.DMA((4,)),
            pltpu.SemaphoreType.DMA((2,)),
            pltpu.SemaphoreType.DMA((2,)),
            pltpu.SemaphoreType.DMA((ITERS, len(PEERS))),
            pltpu.SemaphoreType.DMA((ITERS, len(PEERS))),
        ],
        compiler_params=pltpu.CompilerParams(
            collective_id=0, has_side_effects=True, vmem_limit_bytes=64 * 1024 * 1024
        ),
    )(section_images[0], displacement, fold_mask, tables)
    return both[:2], both[2:]


def solution(mesh):
    in_specs = (P("sec", "row", None), P(None, "sec", "row", None), P(None, "sec", "row", None))
    out_specs = (P(None, "sec", "row", None), P(None, "sec", "row", None))
    return jax.shard_map(
        per_device, mesh=mesh, in_specs=in_specs, out_specs=out_specs, check_vma=False
    )
```

```python
import functools
import math

import jax
import jax.numpy as jnp
import numpy as np
from jax import lax
from jax.experimental import pallas as pl
from jax.experimental.pallas import tpu as pltpu
from jax.sharding import PartitionSpec as P

SIZE = 128
HALF = 64
ITERS = 3
STEP = 0.5
STIFF = 0.2
EPS = 1e-6
SHARP = 0.5 * SIZE
F32 = jnp.float32
BF16 = jnp.bfloat16
COORD = pl.DeviceIdType.MESH

UPPER, LOWER, FAR, BESIDE = 0, 3, 6, 8
SLOTS = 11


def split_table(table):
    high = table.astype(jnp.bfloat16)
    low = (table - high.astype(np.float64)).astype(jnp.bfloat16)
    return high, low


def make_tables():
    index = np.arange(SIZE)
    angles = (index[:, None] * index[None, :] % SIZE) * (2.0 * math.pi / SIZE)
    cosines, sines = np.cos(angles), np.sin(angles)
    sign = np.where(index % 2 == 0, 1.0, -1.0)
    real = cosines[:, :HALF]
    imag = -sines[:, :HALF].copy()
    imag[:, 0] = sign
    zero = np.zeros((SIZE, HALF))
    along_x = np.block([[real, zero, imag, zero], [zero, real, zero, imag]])
    along_u = np.block([[cosines, -sines], [sines, cosines]])
    back_real = 2.0 * cosines[:HALF]
    back_real[0] = 1.0
    back_imag = -2.0 * sines[:HALF]
    back_imag[0] = sign
    wide = np.zeros((HALF, SIZE))
    along_v = np.block(
        [[back_real, wide], [wide, back_real], [back_imag, wide], [wide, back_imag]]
    )
    parts = []
    for table in (along_x, along_u, along_v):
        parts.extend(split_table(table))
    return np.stack(parts)


def fit_even(function, terms):
    nodes = 0.25 * (0.5 + 0.5 * np.cos(np.pi * (np.arange(200) + 0.5) / 200))
    powers = np.vander(nodes * 4.0, terms, increasing=True)
    solved = np.linalg.lstsq(powers, function(np.sqrt(nodes)), rcond=None)[0]
    return [float(c) for c in solved * 4.0 ** np.arange(terms)]


SIN_FIT = fit_even(lambda r: np.sin(np.pi * r) / r, 6)
COS_FIT = fit_even(lambda r: np.cos(np.pi * r), 7)


def horner(coefficients, value):
    total = coefficients[-1]
    for c in coefficients[-2::-1]:
        total = total * value + c
    return total


def turn(turns):
    r = turns - jnp.round(turns)
    squared = r * r
    s = r * horner(SIN_FIT, squared)
    c = horner(COS_FIT, squared)
    return 1.0 - 2.0 * s * s, 2.0 * s * c


def halves(values):
    high = values.astype(BF16)
    return high, (values - high.astype(F32)).astype(BF16)


def dot(a, b):
    return jnp.dot(a, b, preferred_element_type=F32)


def left_product(table, values):
    high, low = halves(values)
    return dot(table[0], high) + (dot(table[0], low) + dot(table[1], high))


def right_product(values, table):
    high, low = halves(values)
    return dot(high, table[0]) + (dot(low, table[0]) + dot(high, table[1]))


def iota(shape, dim):
    return lax.broadcasted_iota(jnp.int32, shape, dim)


def spectrum(image, along_x, along_u):
    rows = jnp.concatenate([image[:, :256], image[:, 256:]], axis=0)
    first = dot(rows, along_x[0]) + dot(rows, along_x[1])
    real = jnp.concatenate([first[:SIZE, :SIZE], first[SIZE:, :SIZE]], axis=1)
    imag = jnp.concatenate([first[:SIZE, SIZE:], first[SIZE:, SIZE:]], axis=1)
    edge = iota((SIZE, 256), 1) % HALF == 0
    main = jnp.concatenate([real, jnp.where(edge, 0.0, -imag)], axis=0)
    last = jnp.where(edge, imag, 0.0)
    full = left_product(along_u, main)
    nyquist = left_product((along_u[0][:, :SIZE], along_u[1][:, :SIZE]), last)
    constant = edge & (iota((SIZE, 256), 0) == 0)
    full_real = jnp.where(constant, 0.0, full[:SIZE])
    full_imag = jnp.where(constant, 0.0, full[SIZE:])
    return full_real, full_imag, nyquist[:SIZE], nyquist[SIZE:]


def column_sums(values):
    middle = values[HALF : HALF + 1]
    return jnp.sum(values, axis=0, keepdims=True) - middle, middle


def energy_rows(spec):
    real, imag, edge_real, edge_imag = spec
    weight = jnp.where(iota((SIZE, 256), 1) % HALF == 0, 1.0, 2.0)
    rows = iota((SIZE, 256), 0)
    out = []
    for power in (weight * (real * real + imag * imag), edge_real * edge_real + edge_imag * edge_imag):
        out.append(jnp.sum(jnp.where(rows == HALF, 0.0, power), axis=0, keepdims=True))
        out.append(power[HALF : HALF + 1])
    return out


def to_lanes(rows):
    lane = iota((rows.shape[0], SIZE), 1)
    left, right = rows[:, :SIZE], rows[:, SIZE:]
    total = jnp.zeros((rows.shape[0], SIZE), F32)
    for c, (part, low) in enumerate([(left, True), (left, False), (right, True), (right, False)]):
        kept = jnp.where((lane < HALF) == low, part, 0.0)
        total = total + jnp.where(lane == c, jnp.sum(kept, axis=1, keepdims=True), 0.0)
    return total


def from_lanes(rows):
    shape = (rows.shape[0], SIZE)
    lane = iota(shape, 1)
    spread = [jnp.broadcast_to(rows[:, c : c + 1], shape) for c in range(4)]
    return jnp.concatenate(
        [
            jnp.where(lane < HALF, spread[0], spread[1]),
            jnp.where(lane < HALF, spread[2], spread[3]),
        ],
        axis=1,
    )


def stack(rows):
    width = rows[0].shape[1]
    pad = -len(rows) % 8
    return jnp.concatenate(rows + [jnp.zeros((1, width), F32)] * pad, axis=0)


def prepare(own, other):
    ar, ai, aer, aei = own
    br, bi, ber, bei = other
    cross_real = ar * br + ai * bi
    cross_imag = ar * bi - ai * br
    edge_real = aer * ber + aei * bei
    edge_imag = aer * bei - aei * ber
    rows = energy_rows(own) + energy_rows(other)
    rows = [row * (1.0 / (SIZE * SIZE)) for row in rows] + [edge_real[HALF : HALF + 1]]
    return cross_real - edge_imag, cross_imag + edge_real, to_lanes(stack(rows))


def sums_of_lags(field_own, field_other, cross_real, cross_imag, terms, along_u, along_v):
    dy_own, dy_other = field_own, field_other
    dx_own = pltpu.roll(field_own, SIZE - 4, 1)
    dx_other = pltpu.roll(field_other, SIZE - 4, 1)
    cosines, _ = turn(
        0.5 * stack([dy_own, dx_own, dy_own + dx_own, dy_other, dx_other, dy_other + dx_other])
    )
    squares = cosines * cosines
    energy_own = terms[0:1] + squares[0:1] * terms[1:2] + squares[1:2] * terms[2:3] + squares[2:3] * terms[3:4]
    energy_other = terms[4:5] + squares[3:4] * terms[5:6] + squares[4:5] * terms[6:7] + squares[5:6] * terms[7:8]
    scale = (SHARP / (SIZE * SIZE)) / jnp.sqrt(energy_own * energy_other + EPS)
    factor_y = cosines[0:1] * cosines[3:4]
    factor_x = cosines[1:2] * cosines[4:5]
    corner = (cosines[2:3] * cosines[5:6] - factor_y * factor_x) * terms[8:9]
    spread = from_lanes(
        stack(
            [
                (dy_own - dy_other) * (-1.0 / SIZE),
                (dx_own - dx_other) * (-1.0 / SIZE),
                factor_y,
                factor_x * scale,
                scale,
                corner * scale,
            ]
        )
    )
    u = iota((SIZE, 256), 0)
    signed_u = jnp.where(u >= HALF, u - SIZE, u).astype(F32)
    turn_cos, turn_sin = turn(signed_u * spread[0:1])
    turn_cos = jnp.where(u == HALF, spread[2:3], turn_cos)
    turn_sin = jnp.where(u == HALF, 0.0, turn_sin)
    shifted = jnp.concatenate(
        [
            cross_real * turn_cos - cross_imag * turn_sin,
            cross_real * turn_sin + cross_imag * turn_cos,
        ],
        axis=0,
    )
    columns = left_product(along_u, shifted)
    real, imag = columns[:SIZE], columns[SIZE:]
    v = iota((1, 256), 1) % HALF
    row_cos, row_sin = turn(v.astype(F32) * spread[1:2])
    row_cos = row_cos * spread[4:5]
    row_sin = row_sin * spread[4:5]
    row_cos_edge = jnp.where(v == 0, spread[3:4], row_cos)
    sign = (1 - 2 * (u % 2)).astype(F32)
    moved_real = real * row_cos - imag * row_sin
    moved_imag = real * row_sin + imag * row_cos_edge + sign * jnp.where(v == 0, spread[5:6], 0.0)
    pairs = jnp.concatenate(
        [
            jnp.concatenate([moved_real[:, :SIZE], moved_imag[:, :SIZE]], axis=1),
            jnp.concatenate([moved_real[:, SIZE:], moved_imag[:, SIZE:]], axis=1),
        ],
        axis=0,
    )
    weights = jnp.exp(right_product(pairs, along_v))

    b = iota((1, 256), 1) % SIZE
    signed_b = jnp.where(b >= HALF, b - SIZE, b).astype(F32)
    totals, moments_a, moments_b, ends_a, ends_b = [], [], [], [], []
    for g in range(2):
        block = weights[g * SIZE : (g + 1) * SIZE]
        total = jnp.sum(block, axis=0, keepdims=True)
        totals.append(total)
        moments_a.append(jnp.sum(block * signed_u, axis=0, keepdims=True))
        moments_b.append(total * signed_b)
        ends_a.append(block[HALF : HALF + 1])
        ends_b.append(jnp.where(b == HALF, total, 0.0))
    rows = stack(totals + moments_a + moments_b + ends_a + ends_b)
    k = iota((16, SIZE), 0)
    lane = iota((16, SIZE), 1)
    kind, g = k // 2, k % 2
    out = [0.0, 0.0, 0.0]
    for which in range(2):
        reduced = jnp.sum(rows[:, which * SIZE : (which + 1) * SIZE], axis=1, keepdims=True)
        here = (lane % 4 == 2 * g + which) & (lane < 8)
        component = lane // 4
        for n, chosen in enumerate(
            (kind == 0, kind == 1 + component, kind == 3 + component)
        ):
            out[n] = out[n] + jnp.sum(jnp.where(here & chosen, reduced, 0.0), axis=0, keepdims=True)
    return out


def kernel(
    images, displacement, fold_mask, tables, result_ref,
    own_image, image, table, disp, mask, first, first_in,
    own_spec, spec, cross, terms, fields, coef, shares, sent, received, raised, raised_in,
    final, final_in,
    load_sem, image_send, image_recv, first_send, first_recv,
    send_sem, row_sem, recv_sem, raised_send, raised_recv, final_sem, go_sem,
):
    section, row = lax.axis_index("sec"), lax.axis_index("row")
    sections, nrows = lax.axis_size("sec"), lax.axis_size("row")
    role = lax.rem(section, 4)
    is0, is1, is2, is3 = role == 0, role == 1, role == 2, role == 3
    works = role != 2
    above, below = section < sections - 1, section > 0
    further = section < sections - 4
    there = {-1: row > 0, 0: None, 1: row < nrows - 1}

    def both(*flags):
        return functools.reduce(jnp.logical_and, [flag for flag in flags if flag is not None])

    def either(*flags):
        return functools.reduce(jnp.logical_or, flags)

    up = jnp.where(is1, 2, 1)
    down = jnp.where(is3, 2, 1)
    any_lower = either(both(is0, below), is1, is3)
    any_upper = either(is0, is1, both(is3, above))

    barrier = pltpu.get_barrier_semaphore()

    def greet(condition, ds, dr):
        @pl.when(both(condition, there[dr]))
        def _():
            pl.semaphore_signal(
                barrier, inc=1, device_id=(section + ds, row + dr), device_id_type=COORD
            )

    for dr in (0, 1, -1):
        greet(any_lower, -down, dr)
        greet(any_upper, up, dr)
        greet(both(is0, below), -3, dr)
        if dr:
            greet(works, 0, dr)
    greet(both(is0, below), -2, 0)
    greet(either(is1, is2), 1, 0)
    greet(is3, -1, 0)

    loads = [
        pltpu.make_async_copy(displacement, disp, load_sem.at[0]),
        pltpu.make_async_copy(fold_mask, mask, load_sem.at[1]),
        pltpu.make_async_copy(images, own_image, load_sem.at[2]),
        pltpu.make_async_copy(tables, table, load_sem.at[3]),
    ]
    for load in loads:
        load.start()
    loads[0].wait()
    loads[1].wait()
    first[...] = jnp.zeros((1, SIZE), F32)
    for k in range(2):
        first[:, 4 * k : 4 * k + 4] = disp[k, 0]
        first[:, 8 + 4 * k : 12 + 4 * k] = mask[k, 0].astype(F32)
    shares[...] = jnp.zeros((2, 2, 1, SIZE), F32)

    def count(flag):
        return flag.astype(jnp.int32)

    beside = count(there[-1]) + count(there[1])
    triple = 1 + beside
    awaited = jnp.where(
        is2,
        2 + count(further),
        beside
        + triple * (count(is1) * (2 + count(further)) + count(is0) * (1 + count(below)))
        + count(is3) * (triple * (1 + count(above)) + 1),
    )
    pl.semaphore_wait(barrier, awaited)

    def image_copy(ds, slot):
        return pltpu.make_async_remote_copy(
            src_ref=images,
            dst_ref=image.at[slot],
            send_sem=image_send.at[ds + 1],
            recv_sem=image_recv.at[slot],
            device_id=(section + ds, row),
            device_id_type=COORD,
        )

    def first_copy(ds, slot):
        return pltpu.make_async_remote_copy(
            src_ref=first,
            dst_ref=first_in.at[slot],
            send_sem=first_send.at[ds + 1],
            recv_sem=first_recv.at[slot],
            device_id=(section + ds, row),
            device_id_type=COORD,
        )

    providing = [(both(is3, above), 1, 0), (is2, -1, 0), (either(is0, is2), 1, 1)]

    def provide(action):
        for condition, ds, slot in providing:
            pl.when(condition)(lambda ds=ds, slot=slot: action(ds, slot))

    def start_both(ds, slot):
        first_copy(ds, slot).start()
        image_copy(ds, slot).start()

    provide(start_both)

    loads[2].wait()
    loads[3].wait()
    along_x, along_u, along_v = (
        (table[0], table[1]), (table[2], table[3]), (table[4], table[5])
    )
    last_image = both(is2, further)

    def put(ref, values):
        for k, value in enumerate(values):
            ref[k] = value

    def get(ref):
        return ref[0], ref[1], ref[2], ref[3]

    @pl.when(works)
    def _():
        put(own_spec, spectrum(own_image[...], along_x, along_u))

    @pl.when(last_image)
    def _():
        pl.semaphore_wait(go_sem, 1)
        image_copy(2, 1).start()

    @pl.when(either(both(is0, below), is1))
    def _():
        first_copy(1, 0).wait_recv()

    @pl.when(either(is1, is3))
    def _():
        first_copy(1, 1).wait_recv()

    @pl.when(both(is0, jnp.logical_not(below)))
    def _():
        first_in[0] = jnp.zeros((1, SIZE), F32)
        for k in range(2):
            image[k] = jnp.zeros((SIZE, 512), BF16)

    lane = iota((1, SIZE), 1)
    column = lane % 4
    inside = lane < 8

    def weights(values, position):
        aligned = pltpu.roll(values, SIZE - 8, 1)
        pair = aligned * jnp.where(
            lane < 4, (position > 0).astype(F32), (position < sections - 1).astype(F32)
        )
        pair = jnp.where(inside, pair, 0.0)
        lower = jnp.where(lane < 4, pair, pltpu.roll(pair, 4, 1))
        upper = jnp.where(lane < 4, pltpu.roll(pair, SIZE - 4, 1), pair)
        norm = STEP / jnp.maximum(lower + upper, 1.0)
        return jnp.where(inside, lower * norm, 0.0), jnp.where(inside, upper * norm, 0.0)

    mine, firsts = first[...], (first_in[0], first_in[1])
    lower_mine, upper_mine = weights(mine, section)
    lower_0, upper_0 = weights(firsts[0], jnp.where(is0, section - 1, section + 1))
    _, upper_1 = weights(firsts[1], section - 1)
    coef[0, 0] = jnp.where(is0, lower_mine, upper_mine)
    coef[0, 1] = jnp.where(is0, upper_0, lower_0)
    coef[1, 0] = jnp.where(is0, lower_0, lower_mine)
    coef[1, 1] = upper_1
    fields[0] = jnp.where(inside, mine, 0.0)
    fields[1] = jnp.where(inside, firsts[0], 0.0)
    fields[2] = jnp.where(inside, firsts[1], 0.0)

    def correlate(slot):
        if slot == 0:
            own, other = fields[0], fields[1]
        else:
            own, other = jnp.where(is0, fields[1], fields[0]), fields[2]
        total, moment, end = sums_of_lags(
            own, other, cross[slot, 0], cross[slot, 1], terms[slot], along_u, along_v
        )
        total = jnp.where(inside, total, 1.0)
        offset = moment / total
        shares[slot, 0] = coef[slot, 0] * offset
        shares[slot, 1] = coef[slot, 1] * (-offset - SIZE * (end / total))

    def ready(slot, own):
        put(spec.at[slot], spectrum(image[slot], along_x, along_u))
        real, imag, sums = prepare(own(), get(spec.at[slot]))
        cross[slot, 0] = real
        cross[slot, 1] = imag
        terms[slot] = sums

    def smooth(rows):
        current = rows[0]
        around = (
            jnp.where(there[-1], rows[-1], 0.0)
            + jnp.where(there[1], rows[1], 0.0)
            + jnp.where(column == 0, 0.0, pltpu.roll(current, 1, 1))
            + jnp.where(column == 3, 0.0, pltpu.roll(current, SIZE - 1, 1))
        )
        return current + STIFF * (around - 4.0 * current)

    def packet(step, ds, dr, slot, port):
        return pltpu.make_async_remote_copy(
            src_ref=sent.at[step],
            dst_ref=received.at[step, slot],
            send_sem=send_sem.at[step, port],
            recv_sem=recv_sem.at[step, slot],
            device_id=(section + ds, row + dr),
            device_id_type=COORD,
        )

    def outgoing(step):
        upwards = (either(is0, both(is3, above)), is0, None)[step]
        downwards = (
            either(both(is0, below), is1, is3),
            either(both(is0, below), is1, is3),
            either(both(is0, below), is1),
        )[step]
        sends = []
        for dr in (0, 1, -1):
            sends.append((both(downwards, there[dr]), -down, dr, UPPER + 1 - dr, 1 + dr))
            if upwards is not None:
                sends.append((both(upwards, there[dr]), 1, dr, LOWER + 1 - dr, 4 + dr))
            if step == 0:
                sends.append((both(is1, further, there[dr]), 3, dr, FAR + 1 - dr, 7 + dr))
        for dr in (1, -1):
            sends.append((both(works, there[dr]), 0, dr, None, None))
        return sends

    def row_packet(step, dr):
        k = (1 - dr) // 2
        return pltpu.make_async_remote_copy(
            src_ref=sent.at[step],
            dst_ref=received.at[step, BESIDE + 1 + k],
            send_sem=row_sem.at[step, k],
            recv_sem=recv_sem.at[step, BESIDE + 1 + k],
            device_id=(section, row + dr),
            device_id_type=COORD,
        )

    def act_on(step, method):
        for condition, ds, dr, slot, port in outgoing(step):
            def act(ds=ds, dr=dr, slot=slot, port=port):
                copy = row_packet(step, dr) if slot is None else packet(step, ds, dr, slot, port)
                getattr(copy, method)()

            pl.when(condition)(act)

    def raise_packet(step, dr):
        return pltpu.make_async_remote_copy(
            src_ref=raised.at[step],
            dst_ref=raised_in.at[step, 1 - dr],
            send_sem=raised_send.at[step, 1 - dr],
            recv_sem=raised_recv.at[step, 1 - dr],
            device_id=(section + 2, row + dr),
            device_id_type=COORD,
        )

    def incoming(step):
        uppers = (any_upper, any_upper, either(is0, both(is3, above)))[step]
        for dr in (0, 1, -1):
            slots = [(both(uppers, there[dr]), UPPER + 1 + dr)]
            if step == 0:
                slots.append((both(is0, below, there[dr]), LOWER + 1 + dr))
                slots.append((both(is0, below, there[dr]), FAR + 1 + dr))
            for condition, slot in slots:
                pl.when(condition)(lambda slot=slot: packet(step, 1, 0, slot, 0).wait_recv())
        for dr in (1, -1):
            pl.when(both(works, there[-dr]))(lambda dr=dr: row_packet(step, dr).wait_recv())

    def incoming_lower(step):
        for dr in (0, 1, -1):
            if step < ITERS - 1:
                pl.when(both(is1, there[dr]))(
                    lambda dr=dr: packet(step, 1, 0, LOWER + 1 + dr, 0).wait_recv()
                )
            pl.when(both(is3, there[dr]))(lambda dr=dr: raise_packet(step, -dr).wait_recv())

    def correlate_0(step):
        correlate(0)

        @pl.when(is1)
        def _():
            raised[step] = shares[0, 1]
            for dr in (0, 1, -1):
                action = raise_packet(step, dr).start
                action() if dr == 0 else pl.when(there[dr])(action)

    finish_lower = None
    for step in range(ITERS):
        if step == 0:
            @pl.when(either(is1, is3))
            def _():
                image_copy(1, 1).wait_recv()
                ready(1, lambda: get(own_spec))
                correlate(1)

            @pl.when(either(both(is0, below), is1))
            def _():
                image_copy(1, 0).wait_recv()

            @pl.when(either(is0, is1))
            def _():
                ready(0, lambda: get(own_spec))
                correlate_0(0)
        else:
            pl.when(either(is0, is1))(lambda: correlate_0(step))
            finish_lower()
            pl.when(works if step == 1 else either(is1, is3))(lambda: correlate(1))

        field, field_0, field_1 = fields[0], fields[1], fields[2]
        own_0, other_0, own_1, other_1 = shares[0, 0], shares[0, 1], shares[1, 0], shares[1, 1]
        sent[step, 0] = field + own_0 + jnp.where(is0, 0.0, own_1)
        sent[step, 1] = jnp.where(is0, other_0, jnp.where(is1, other_1, field_1 + other_1))
        sent[step, 2] = jnp.where(is1, other_0, field_0 + other_0 + own_1)
        act_on(step, "start")

        if step == 0:
            @pl.when(both(is3, above))
            def _():
                image_copy(1, 0).wait_send()
                pl.semaphore_signal(
                    go_sem, inc=1, device_id=(section - 1, row), device_id_type=COORD
                )

            @pl.when(is0)
            def _():
                @pl.when(below)
                def _():
                    image_copy(1, 1).wait_recv()

                ready(1, lambda: get(spec.at[0]))

        incoming(step)

        def beside_row(kind, dr, step=step):
            if dr == 0:
                return sent[step, kind]
            return received[step, BESIDE + 1 + (1 + dr) // 2, kind]

        def from_channel(channel, kind, dr, step=step):
            return received[step, channel + 1 + dr, kind]

        rows = (-1, 0, 1)
        takes_upper = either(is0, both(is3, above))
        from_upper = {
            dr: jnp.where(takes_upper, from_channel(UPPER, 1, dr), 0.0) for dr in rows
        }
        smoothed = smooth({dr: beside_row(0, dr) + from_upper[dr] for dr in rows})
        if step == ITERS - 1:
            mean = (own_0 + jnp.where(is0, 0.0, own_1) + from_upper[0]) * (1.0 / STEP)
            incoming_lower(step)

            @pl.when(is3)
            def _():
                final[0] = smooth({dr: beside_row(1, dr) + raised_in[step, 1 + dr] for dr in rows})
                final[1] = (other_1 + raised_in[step, 1]) * (1.0 / STEP)
        else:
            bounded = jnp.logical_or(below, jnp.logical_not(is0))
            fields[0] = jnp.where(inside, smoothed, 0.0)

            @pl.when(is0)
            def _():
                if step == 0:
                    known = {dr: from_channel(LOWER, 0, dr) + beside_row(1, dr) for dr in rows}
                else:
                    known = {dr: beside_row(2, dr) for dr in rows}
                fields[1] = jnp.where(jnp.logical_and(inside, below), smooth(known), 0.0)

            @pl.when(is1)
            def _():
                known = {dr: from_channel(UPPER, 1, dr) + beside_row(2, dr) for dr in rows}
                fields[1] = jnp.where(inside, smooth(known), 0.0)

            def finish_lower(step=step, beside_row=beside_row, from_channel=from_channel):
                incoming_lower(step)
                far = {
                    dr: beside_row(1, dr)
                    + jnp.where(is1, from_channel(LOWER, 0, dr), raised_in[step, 1 + dr])
                    for dr in rows
                }
                if step == 0:
                    far = {
                        dr: jnp.where(
                            is0, from_channel(LOWER, 1, dr) + from_channel(FAR, 2, dr), far[dr]
                        )
                        for dr in rows
                    }
                fields[2] = jnp.where(jnp.logical_and(inside, bounded), smooth(far), 0.0)

    final_copy = pltpu.make_async_remote_copy(
        src_ref=final,
        dst_ref=final_in,
        send_sem=final_sem.at[0],
        recv_sem=final_sem.at[1],
        device_id=(section - 1, row),
        device_id_type=COORD,
    )

    def finish(relaxed_row, mean_row):
        for k in range(2):
            result_ref[k, 0] = relaxed_row[:, 4 * k : 4 * k + 4]
            result_ref[2 + k, 0] = mean_row[:, 4 * k : 4 * k + 4]

    pl.when(is3)(final_copy.start)
    pl.when(works)(lambda: finish(smoothed, mean))

    @pl.when(is2)
    def _():
        final_copy.wait_recv()
        finish(final_in[0], final_in[1])

    pl.when(is3)(final_copy.wait_send)

    def sent_both(ds, slot):
        first_copy(ds, slot).wait_send()
        if (ds, slot) != (1, 0):
            image_copy(ds, slot).wait_send()

    provide(sent_both)
    pl.when(last_image)(lambda: image_copy(2, 1).wait_send())
    for step in range(ITERS):
        act_on(step, "wait_send")
        for dr in (0, 1, -1):
            pl.when(both(is1, there[dr]))(
                lambda step=step, dr=dr: raise_packet(step, dr).wait_send()
            )


def per_device(section_images, displacement, fold_mask):
    tables = jnp.asarray(make_tables())
    result = jax.ShapeDtypeStruct((4, 1, 1, 4), F32)
    both = pl.pallas_call(
        kernel,
        out_shape=result,
        in_specs=[pl.BlockSpec(memory_space=pltpu.HBM)] * 4,
        out_specs=pl.BlockSpec(memory_space=pltpu.VMEM),
        scratch_shapes=[
            pltpu.VMEM((SIZE, 512), BF16),
            pltpu.VMEM((2, SIZE, 512), BF16),
            pltpu.VMEM((6, 256, 256), BF16),
            pltpu.VMEM((2, 1, 1, 4), F32),
            pltpu.VMEM((2, 1, 1, 4), jnp.int32),
            pltpu.VMEM((1, SIZE), F32),
            pltpu.VMEM((2, 1, SIZE), F32),
            pltpu.VMEM((4, SIZE, 256), F32),
            pltpu.VMEM((2, 4, SIZE, 256), F32),
            pltpu.VMEM((2, 2, SIZE, 256), F32),
            pltpu.VMEM((2, 16, SIZE), F32),
            pltpu.VMEM((3, 1, SIZE), F32),
            pltpu.VMEM((2, 2, 1, SIZE), F32),
            pltpu.VMEM((2, 2, 1, SIZE), F32),
            pltpu.VMEM((ITERS, 3, 1, SIZE), F32),
            pltpu.VMEM((ITERS, SLOTS, 3, 1, SIZE), F32),
            pltpu.VMEM((ITERS, 1, SIZE), F32),
            pltpu.VMEM((ITERS, 3, 1, SIZE), F32),
            pltpu.VMEM((2, 1, SIZE), F32),
            pltpu.VMEM((2, 1, SIZE), F32),
            pltpu.SemaphoreType.DMA((4,)),
            pltpu.SemaphoreType.DMA((4,)),
            pltpu.SemaphoreType.DMA((2,)),
            pltpu.SemaphoreType.DMA((4,)),
            pltpu.SemaphoreType.DMA((2,)),
            pltpu.SemaphoreType.DMA((ITERS, 9)),
            pltpu.SemaphoreType.DMA((ITERS, 2)),
            pltpu.SemaphoreType.DMA((ITERS, SLOTS)),
            pltpu.SemaphoreType.DMA((ITERS, 3)),
            pltpu.SemaphoreType.DMA((ITERS, 3)),
            pltpu.SemaphoreType.DMA((2,)),
            pltpu.SemaphoreType.REGULAR,
        ],
        compiler_params=pltpu.CompilerParams(
            collective_id=0, has_side_effects=True, vmem_limit_bytes=64 * 1024 * 1024
        ),
    )(section_images[0], displacement, fold_mask, tables)
    return both[:2], both[2:]


def solution(mesh):
    in_specs = (P("sec", "row", None), P(None, "sec", "row", None), P(None, "sec", "row", None))
    out_specs = (P(None, "sec", "row", None), P(None, "sec", "row", None))
    return jax.shard_map(
        per_device, mesh=mesh, in_specs=in_specs, out_specs=out_specs, check_vma=False
    )
```
